256 devices in a mesh: tm: 32 (over y_lo, z, core), net: 8 (over x, y_hi).
Axes of the slice: x: 4, y: 4 (y_hi: 2, y_lo: 2; y = y_hi * 2 + y_lo), z: 8, core: 2. Of those that a mesh axis runs over, the one named last changes fastest.
Arguments:
- demand: float32 [4096, 12288], P('net', 'tm'), may hold values from 0.5 to 1.5
- availability: float32 [4096, 12288], P('net', 'tm'), may hold values from 0.05 to 1
- gen_cost: float32 [4096], P('net'), may hold values from 0.2 to 2
- cap_cost: float32 [4096], P('net'), may hold values from 1228.8 to 7372.8
- runoff: bfloat16 [32768, 12288], P('net', 'tm'), may hold values from 0.0099487305 to 1
- cell_plant: int32 [32768], P('net'), may hold values from 0 to 1799, as said below
- plant_bus: int32 [1800], P('net'), may hold values from 0 to 511
- store_cap: float32 [1800], P('net'), may hold values from 1 to 4
- line_from: int32 [5120], P('net'), may hold values from 0 to 511
- line_to: int32 [5120], P('net'), may hold values from 0 to 511
- line_cap: float32 [5120], P('net'), may hold values from 0.5 to 2
- cut_from: int32 [1024], P('net'), may hold values from 0 to 511
- cut_to: int32 [1024], P('net'), may hold values from 0 to 511
- cut_cap: float32 [1024], P('net'), may hold values from 0.5 to 2
- generation: float32 [4096, 12288], P('net', 'tm'), may hold values from 0 to 2
- capacity: float32 [4096], P('net'), may hold values from 0.05 to 2
- release: float32 [1800, 12288], P('net', 'tm'), may hold values from 0 to 1
- storage_level: float32 [1800, 12288], P('net', 'tm'), may hold values from 0 to 2
- line_flow: float32 [5120, 12288], P('net', 'tm'), may hold values from -6 to 6
- cut_flow: float32 [1024, 12288], P('net', 'tm'), may hold values from -6 to 6
- dual_bal: float32 [4096, 12288], P('net', 'tm'), may hold values from -6 to 6
- dual_cap: float32 [4096, 12288], P('net', 'tm'), may hold values from 0 to 2.25, as said below
- dual_sto: float32 [1800, 12288], P('net', 'tm'), may hold values from -6 to 6
Outputs:
- new_generation: float32 [4096, 12288], P('net', 'tm')
- new_capacity: float32 [4096], P('net')
- new_release: float32 [1800, 12288], P('net', 'tm')
- new_level: float32 [1800, 12288], P('net', 'tm')
- new_flow: float32 [5120, 12288], P('net', 'tm')
- new_cut_flow: float32 [1024, 12288], P('net', 'tm')
- new_dual_bal: float32 [4096, 12288], P('net', 'tm')
- new_dual_cap: float32 [4096, 12288], P('net', 'tm')
- new_dual_sto: float32 [1800, 12288], P('net', 'tm')
The draws below stay inside these ranges and needn't reach their ends.
Inputs may be any that keep to these rules, and one draw needn't show every extreme that they name: `cell_plant`: plant numbers; cell c lies in zone floor(c / 4096) and drains into a plant of that zone, of the zone before it or of the zone after it (zones taken cyclically, plant p in zone floor(p / 225)). `plant_bus`: bus numbers within the plant's zone. `line_from`: bus numbers within the line's zone. `line_to`: bus numbers within the line's zone. `cut_from`: bus numbers within the cut line's own zone. `dual_cap`: nonnegative.
All inputs are finite; a program needn't handle non-finite values.
Results may differ from the reference program's by a relative error of at most 0.0003.
Values sent between devices are 32-bit elements; how exact they have to be, the bound alone decides.
A program may use at most 64 MiB of HBM per device.

```python
import math
import jax
import jax.numpy as jnp

BUSES = 4096
PLANTS = 1800
CELL_DEV = 4096
ITERS = 2
ZONES = 8
BUS_DEV = 512
PLANT_DEV = 225
LOC_LINES = 640
CUT_LINES = 128
HOURS = 12288
CELLS = 32768


def draw_dual_cap(key, part):
    hour_frac = jnp.arange(HOURS, dtype=jnp.float32) / HOURS
    growth = 0.5 + hour_frac
    values = jax.random.uniform(key, (BUSES, HOURS), dtype=jnp.float32, minval=0.0, maxval=1.0)
    return values * growth[None, :]


def draw_cell_plant(key, part):
    key_kind = jax.random.fold_in(key, 11)
    key_local = jax.random.fold_in(key, 13)
    cell_ids = jnp.arange(CELLS, dtype=jnp.int32)
    cell_zone = cell_ids // CELL_DEV
    within = cell_ids % CELL_DEV
    kind = jax.random.randint(key_kind, (CELLS,), 0, 4)
    side = jnp.where(kind == 0, -1, jnp.where(kind == 1, 1, 0)).astype(jnp.int32)
    side = jnp.where(within == 0, -1, jnp.where(within == 1, 1, side)).astype(jnp.int32)
    target = (cell_zone + side + ZONES) % ZONES
    local = jax.random.randint(key_local, (CELLS,), 0, PLANT_DEV)
    return (target * PLANT_DEV + local).astype(jnp.int32)


def place_ends(drawn, own_key, least, largest):
    longest = drawn.shape.index(max(drawn.shape))
    spots = []
    for shift in (0, 1):
        where = [jax.random.randint(jax.random.fold_in(own_key, axis), (), 0, length) for axis, length in enumerate(drawn.shape)]
        where[longest] = (where[longest] + shift) % drawn.shape[longest]
        spots.append(tuple(where))
    return drawn.at[spots[0]].set(least).at[spots[1]].set(largest)


def level_of(key, shape, pieces, smallest, high):
    def one(axis_at, blocks):
        steps = jax.random.uniform(jax.random.fold_in(jax.random.fold_in(key, 6), axis_at), (blocks,), jnp.float32, smallest / len(pieces), high / len(pieces))
        return jnp.repeat(jnp.exp(steps), shape[axis_at] // blocks).reshape((-1,) + (1,) * (len(shape) - axis_at - 1))

    level = one(*pieces[0])
    for cut in pieces[1:]:
        level = level * one(*cut)
    return level


def normal_values(stream_key, dims, deviation, most, split=(), kind=jnp.bfloat16):
    result = jax.random.normal(stream_key, dims, jnp.float32) * deviation
    if len(split) > 0:
        result = level_of(stream_key, dims, split, -0.22, 0.18) * result
    return jnp.clip(result, min=-most, max=most).astype(kind)


def setup_inputs(seed: int = 0) -> dict:
    splits = jax.random.split(jax.random.key(seed), 24)
    return {
        "demand": jnp.clip(0.5 + 1.0 * jax.random.uniform(splits[0], (BUSES, HOURS), jnp.float32) ** level_of(splits[0], (BUSES, HOURS), ((0, 8), (1, 32)), -0.2, 0.2), 0.5, 1.5),
        "availability": jnp.clip(0.05 + 0.95 * jax.random.uniform(splits[1], (BUSES, HOURS), jnp.float32) ** level_of(splits[1], (BUSES, HOURS), ((0, 8), (1, 32)), -0.2, 0.2), 0.05, 1.0),
        "gen_cost": jnp.clip(jnp.exp(math.log(2.0) - 2.3025851 * jax.random.uniform(splits[2], (BUSES,), jnp.float32) ** level_of(splits[2], (BUSES,), ((0, 8),), -0.2, 0.2)), 0.2, 2.0),
        "cap_cost": jnp.clip(jnp.exp(math.log(7372.8) - 1.7917594 * jax.random.uniform(splits[3], (BUSES,), jnp.float32) ** level_of(splits[3], (BUSES,), ((0, 8),), -0.2, 0.2)), 1228.8, 7372.8),
        "runoff": jnp.clip(jnp.exp(math.log(1.0) - 4.61031033 * jax.random.uniform(splits[4], (CELLS, HOURS), jnp.float32) ** level_of(splits[4], (CELLS, HOURS), ((0, 8), (1, 32)), -0.2, 0.2)), 0.0099487305, 1.0).astype(jnp.bfloat16),
        "cell_plant": draw_cell_plant(jax.random.fold_in(splits[23], 71), 0),
        "plant_bus": place_ends(jax.random.randint(splits[6], (PLANTS,), 0, BUS_DEV), jax.random.fold_in(splits[6], 1), 0, BUS_DEV - 1).astype(jnp.int32),
        "store_cap": jnp.clip(jnp.exp(math.log(4.0) - 1.3862944 * jax.random.uniform(splits[7], (PLANTS,), jnp.float32) ** level_of(splits[7], (PLANTS,), ((0, 8),), -0.2, 0.2)), 1.0, 4.0),
        "line_from": place_ends(jax.random.randint(splits[8], (LOC_LINES * ZONES,), 0, BUS_DEV), jax.random.fold_in(splits[8], 1), 0, BUS_DEV - 1).astype(jnp.int32),
        "line_to": place_ends(jax.random.randint(splits[9], (LOC_LINES * ZONES,), 0, BUS_DEV), jax.random.fold_in(splits[9], 1), 0, BUS_DEV - 1).astype(jnp.int32),
        "line_cap": jnp.clip(jnp.exp(math.log(2.0) - 1.3862944 * jax.random.uniform(splits[10], (LOC_LINES * ZONES,), jnp.float32) ** level_of(splits[10], (LOC_LINES * ZONES,), ((0, 8),), -0.2, 0.2)), 0.5, 2.0),
        "cut_from": place_ends(jax.random.randint(splits[11], (CUT_LINES * ZONES,), 0, BUS_DEV), jax.random.fold_in(splits[11], 1), 0, BUS_DEV - 1).astype(jnp.int32),
        "cut_to": place_ends(jax.random.randint(splits[12], (CUT_LINES * ZONES,), 0, BUS_DEV), jax.random.fold_in(splits[12], 1), 0, BUS_DEV - 1).astype(jnp.int32),
        "cut_cap": jnp.clip(jnp.exp(math.log(2.0) - 1.3862944 * jax.random.uniform(splits[13], (CUT_LINES * ZONES,), jnp.float32) ** level_of(splits[13], (CUT_LINES * ZONES,), ((0, 8),), -0.2, 0.2)), 0.5, 2.0),
        "generation": jnp.clip(2.0 * jax.random.uniform(splits[14], (BUSES, HOURS), jnp.float32) ** level_of(splits[14], (BUSES, HOURS), ((0, 8), (1, 32)), -0.2, 0.2), 0.0, 2.0),
        "capacity": jnp.clip(jnp.exp(math.log(2.0) - 3.6888794 * jax.random.uniform(splits[15], (BUSES,), jnp.float32) ** level_of(splits[15], (BUSES,), ((0, 8),), -0.2, 0.2)), 0.05, 2.0),
        "release": jnp.clip(1.0 * jax.random.uniform(splits[16], (PLANTS, HOURS), jnp.float32) ** level_of(splits[16], (PLANTS, HOURS), ((0, 8), (1, 32)), -0.2, 0.2), 0.0, 1.0),
        "storage_level": jnp.clip(2.0 * jax.random.uniform(splits[17], (PLANTS, HOURS), jnp.float32) ** level_of(splits[17], (PLANTS, HOURS), ((0, 8), (1, 32)), -0.2, 0.2), 0.0, 2.0),
        "line_flow": normal_values(splits[18], (LOC_LINES * ZONES, HOURS), 1.0, 6.0, ((0, 8), (1, 32)), jnp.float32),
        "cut_flow": normal_values(splits[19], (CUT_LINES * ZONES, HOURS), 1.0, 6.0, ((0, 8), (1, 32)), jnp.float32),
        "dual_bal": normal_values(splits[20], (BUSES, HOURS), 1.0, 6.0, ((0, 8), (1, 32)), jnp.float32),
        "dual_cap": draw_dual_cap(jax.random.fold_in(splits[23], 71), 0),
        "dual_sto": normal_values(splits[22], (PLANTS, HOURS), 1.0, 6.0, ((0, 8), (1, 32)), jnp.float32),
    }


primal_step = 0.4
dual_step = 0.4


def clipped(values, bound):
    return jnp.minimum(jnp.maximum(values, -bound), bound)


def reference(demand, availability, gen_cost, cap_cost, runoff, cell_plant, plant_bus, store_cap, line_from, line_to, line_cap, cut_from, cut_to, cut_cap, generation, capacity, release, storage_level, line_flow, cut_flow, dual_bal, dual_cap, dual_sto):
    inflow = jax.ops.segment_sum(runoff.astype(jnp.float32), cell_plant, num_segments=PLANTS)
    plant_zone = jnp.arange(PLANTS, dtype=jnp.int32) // PLANT_DEV
    plant_home = (plant_bus + BUS_DEV * plant_zone).astype(jnp.int32)
    line_zone = jnp.arange(LOC_LINES * ZONES, dtype=jnp.int32) // LOC_LINES
    from_bus = (line_from + BUS_DEV * line_zone).astype(jnp.int32)
    to_bus = (line_to + BUS_DEV * line_zone).astype(jnp.int32)
    cut_zone = jnp.arange(CUT_LINES * ZONES, dtype=jnp.int32) // CUT_LINES
    cut_start = (cut_from + BUS_DEV * cut_zone).astype(jnp.int32)
    cut_end = (cut_to + BUS_DEV * ((cut_zone + 1) % ZONES)).astype(jnp.int32)
    cap_step = primal_step / HOURS
    for iteration in range(ITERS):
        cap_price = jnp.sum(availability * dual_cap, axis=1)
        cap_next = jnp.maximum(0.0, capacity - cap_step * (cap_cost - cap_price))
        gen_next = jnp.maximum(0.0, generation - primal_step * (gen_cost[:, None] - dual_bal + dual_cap))
        rel_next = jnp.maximum(0.0, release + primal_step * (dual_bal[plant_home] + dual_sto))
        sto_after = jnp.roll(dual_sto, -1, axis=1)
        level_next = jnp.minimum(jnp.maximum(storage_level + primal_step * (dual_sto - sto_after), 0.0), store_cap[:, None])
        flow_next = clipped(line_flow + primal_step * (dual_bal[to_bus] - dual_bal[from_bus]), line_cap[:, None])
        cut_next = clipped(cut_flow + primal_step * (dual_bal[cut_end] - dual_bal[cut_start]), cut_cap[:, None])
        gen_bar = 2.0 * gen_next - generation
        cap_bar = 2.0 * cap_next - capacity
        rel_bar = 2.0 * rel_next - release
        level_bar = 2.0 * level_next - storage_level
        flow_bar = 2.0 * flow_next - line_flow
        cut_bar = 2.0 * cut_next - cut_flow
        balance = gen_bar + jax.ops.segment_sum(rel_bar, plant_home, num_segments=BUSES)
        balance = balance + jax.ops.segment_sum(flow_bar, to_bus, num_segments=BUSES) - jax.ops.segment_sum(flow_bar, from_bus, num_segments=BUSES)
        balance = balance + jax.ops.segment_sum(cut_bar, cut_end, num_segments=BUSES) - jax.ops.segment_sum(cut_bar, cut_start, num_segments=BUSES)
        bal_next = dual_bal + dual_step * (demand - balance)
        dcap_next = jnp.maximum(0.0, dual_cap - dual_step * (availability * cap_bar[:, None] - gen_bar))
        level_before = jnp.roll(level_bar, 1, axis=1)
        dsto_next = dual_sto + dual_step * (inflow - level_bar + level_before - rel_bar)
        generation, capacity, release, storage_level = gen_next, cap_next, rel_next, level_next
        line_flow, cut_flow = flow_next, cut_next
        dual_bal, dual_cap, dual_sto = bal_next, dcap_next, dsto_next
    return (generation, capacity, release, storage_level, line_flow, cut_flow, dual_bal, dual_cap, dual_sto)
```

```python
import jax
import jax.numpy as jnp
from jax import lax
from jax.experimental import pallas as pl
from jax.experimental.pallas import tpu as pltpu
from jax.sharding import PartitionSpec as P

MESH = pl.DeviceIdType.MESH
PRIMAL = 0.4
DUAL = 0.4
W = 128
F32 = jnp.float32
BF16 = jnp.bfloat16


def split(values):
    hi = values.astype(BF16)
    lo = (values - hi.astype(F32)).astype(BF16)
    return jnp.concatenate([hi, lo], axis=1)


def joined(product):
    return product[:, :W] + product[:, W:]


def dot(a, b):
    return jnp.dot(a, b, preferred_element_type=F32)


def columns(row):
    blocks = []
    for i in range(row.shape[1] // W):
        blocks.append(jnp.transpose(jnp.broadcast_to(row[:, i * W : (i + 1) * W], (W, W))))
    return jnp.concatenate(blocks, axis=0) if len(blocks) > 1 else blocks[0]


def wide(block, count):
    return jnp.concatenate([block] * count, axis=1) if count > 1 else block


def make_kernel(sizes):
    buses, plants, lines, cuts, cells, hours, times, zones = sizes
    chunks = hours // W
    pad = -(-plants // W) * W
    prow = -(-plants // 16) * 16
    srow = -(-plants // 8) * 8
    parts = 4
    depth = cells // parts
    L0, F0, T0, P0 = 0, lines, lines + cuts, lines + 2 * cuts
    rows = P0 + pad
    i_to, i_from, i_cf, i_ct, i_pl = 0, lines, 2 * lines, 2 * lines + cuts, 2 * lines + 2 * cuts
    c_gen, c_line, c_cut, c_sto = 0, buses, buses + lines, buses + lines + cuts
    r_cost, r_cap = c_sto + pad, c_sto + pad + buses
    cap_step = PRIMAL / (hours * times)

    def kernel(
        ints, floats, cell,
        h_dem, h_av, h_run, h_gen, h_rel, h_lev, h_lf, h_cf, h_bal, h_dc, h_ds,
        o_gen, o_cap, o_rel, o_lev, o_lf, o_cf, o_bal, o_dc, o_ds,
        dem, av, run, gen, rel, lev, lf, cf, bal, dc, ds,
        inc, inct, bars, gbar, lbar, colf, padr, dcut, far, near, own,
        x_ct, x_ds, x_lb, s_p, x_p, s_b, x_b, x_far, x_inf, slots,
        isem, ct_s, ct_r, ds_s, ds_r, lb_s, lb_r, p_s, p_r, b_s, b_r, far_s, far_r, inf_s, inf_r, ps_s, ps_r,
    ):
        t = lax.axis_index("tm")
        q = lax.axis_index("net")
        qn = lax.rem(q + 1, zones)
        qp = lax.rem(q + zones - 1, zones)
        sign = 1 - 2 * lax.rem(q, 2)
        mate = q + sign
        far_zone = lax.rem(q - sign + zones, zones)
        far_to = lax.rem(q - 2 * sign + zones, zones)
        tn = lax.rem(t + 1, times)
        tp = lax.rem(t + times - 1, times)

        loads = {}
        pairs = [
            ("ds", h_ds, ds), ("bal", h_bal, bal), ("av", h_av, av), ("dc", h_dc, dc),
        ]
        for k in range(parts):
            at = pl.ds(k * depth, depth)
            pairs.append((("run", k), h_run.at[at], run.at[at]))
        pairs += [
            ("cf", h_cf, cf), ("lf", h_lf, lf), ("rel", h_rel, rel), ("gen", h_gen, gen),
            ("lev", h_lev, lev), ("dem", h_dem, dem),
        ]
        for n, (name, src, dst) in enumerate(pairs):
            loads[name] = pltpu.make_async_copy(src, dst, isem.at[n])
            loads[name].start()

        barrier = pltpu.get_barrier_semaphore()

        def greet(i, carry):
            pl.semaphore_signal(
                barrier, inc=1, device_id=(lax.rem(t + i, times), q), device_id_type=MESH
            )
            return carry

        lax.fori_loop(1, times, greet, 0)
        for d in (1, 2, zones - 2, zones - 1):
            pl.semaphore_signal(
                barrier, inc=1, device_id=(t, lax.rem(q + d, zones)), device_id_type=MESH
            )
        pl.semaphore_wait(barrier, times + 3)

        sent = []

        def send(src, dst, ssem, rsem, tt, qq):
            copy = pltpu.make_async_remote_copy(
                src_ref=src, dst_ref=dst, send_sem=ssem, recv_sem=rsem,
                device_id=(tt, qq), device_id_type=MESH,
            )
            copy.start()
            sent.append(copy)
            return copy

        def lanes(c):
            return slice(c * W, (c + 1) * W)

        k_ct = send(ints.at[:, pl.ds(i_ct, cuts)], x_ct, ct_s, ct_r, t, qn)
        loads["ds"].wait()
        k_ds = [send(ds.at[:, pl.ds(0, W)], x_ds.at[0], ds_s.at[0], ds_r.at[0], tp, q)]

        def price_out(k, dual_of):
            total = None
            for c in range(chunks):
                term = av[:, lanes(c)] * dual_of(c)
                total = term if total is None else total + term
            row = jnp.concatenate(
                [
                    jnp.sum(jnp.transpose(total[i * W : (i + 1) * W]), axis=0, keepdims=True)
                    for i in range(buses // W)
                ],
                axis=1,
            )
            slots[k, 0] = row

            def out(i, carry):
                pltpu.make_async_remote_copy(
                    src_ref=slots.at[k, 0], dst_ref=slots.at[k, i],
                    send_sem=ps_s.at[k], recv_sem=ps_r.at[k],
                    device_id=(lax.rem(t + i, times), q), device_id_type=MESH,
                ).start()
                return carry

            lax.fori_loop(1, times, out, 0)

        def price_all(k):
            everyone = slots.at[k, pl.ds(1, times - 1)]
            whole = pltpu.make_async_remote_copy(
                src_ref=everyone, dst_ref=everyone, send_sem=ps_s.at[k], recv_sem=ps_r.at[k],
                device_id=(tn, q), device_id_type=MESH,
            )
            whole.wait_recv()
            total = slots[k, lax.rem(t + times, times)]
            for j in range(1, times):
                total = total + slots[k, lax.rem(t - j + times, times)]
            whole.wait_send()
            return total

        loads["av"].wait()
        loads["dc"].wait()
        price_out(0, lambda c: dc[:, lanes(c)])

        lane_bus = lax.broadcasted_iota(jnp.int32, (W, buses), 1)
        row_bus = lax.broadcasted_iota(jnp.int32, (buses, W), 0)
        one, zero = F32(1.0), F32(0.0)

        def flags(mask):
            return jnp.where(mask, one, zero)

        def place(at, to_row, from_row):
            m = jnp.zeros((W, buses), F32)
            mt = jnp.zeros((buses, W), F32)
            if to_row is not None:
                m = m + flags(wide(columns(to_row), buses // W) == lane_bus)
                mt = mt + flags(to_row == row_bus)
            if from_row is not None:
                m = m - flags(wide(columns(from_row), buses // W) == lane_bus)
                mt = mt - flags(from_row == row_bus)
            inc[at : at + W, :] = m.astype(BF16)
            inct[:, at : at + W] = mt.astype(BF16)

        for i in range(lines // W):
            place(
                L0 + i * W,
                ints[:, i_to + i * W : i_to + (i + 1) * W],
                ints[:, i_from + i * W : i_from + (i + 1) * W],
            )
        for i in range(cuts // W):
            place(F0 + i * W, None, ints[:, i_cf + i * W : i_cf + (i + 1) * W])
        for i in range(pad // W):
            place(P0 + i * W, ints[:, i_pl + i * W : i_pl + (i + 1) * W], None)
        for i in range(r_cost // W):
            colf[i * W : (i + 1) * W, :] = columns(floats[:, i * W : (i + 1) * W])
        padr[...] = jnp.zeros_like(padr)

        k_ct.wait_recv()
        for i in range(cuts // W):
            place(T0 + i * W, x_ct[:, i * W : (i + 1) * W], None)

        loads["bal"].wait()
        k_p, k_b = [], []

        def send_prices(k, c, value):
            s_p[k, c] = joined(dot(inc[T0:P0, :], value))
            k_p.append(send(s_p.at[k, c], x_p.at[k, c], p_s.at[k, c], p_r.at[k, c], t, qp))

        for c in range(chunks):
            send_prices(0, c, split(bal[:, lanes(c)]))

        def terms(zone, out):
            ids = lax.broadcasted_iota(jnp.int32, (prow, depth), 0) + zone * plants
            total = None
            for k in range(parts):
                if ("run", k) in loads:
                    loads.pop(("run", k)).wait()
                onehot = flags(ids == cell[:, k * depth : (k + 1) * depth]).astype(BF16)
                term = dot(onehot, run[k * depth : (k + 1) * depth, :])
                total = term if total is None else total + term
            for c in range(chunks):
                out[c] = total[:, lanes(c)]

        terms(far_zone, far)
        k_far = [
            send(far.at[c, pl.ds(0, srow)], x_far.at[c], far_s.at[c], far_r.at[c], t, far_to)
            for c in range(chunks)
        ]

        loads["cf"].wait()
        loads["lf"].wait()
        loads["rel"].wait()

        def bound(v, b):
            return jnp.minimum(jnp.maximum(v, -b), b)

        def line_step(c, value, flow, flow_out):
            diff = joined(dot(inc[L0:T0, :], value))
            cap = colf[c_line : c_line + lines, :]
            old = flow[:, lanes(c)]
            new = bound(old + PRIMAL * diff[:lines], cap)
            bars[c, L0 : L0 + lines, :] = split(2.0 * new - old)
            flow_out[:, lanes(c)] = new
            dcut[:, lanes(c)] = diff[lines:]

        def cut_step(k, c, flow, flow_out):
            k_p[k * chunks + c].wait_recv()
            cap = colf[c_cut : c_cut + cuts, :]
            old = flow[:, lanes(c)]
            new = bound(old + PRIMAL * (x_p[k, c] + dcut[:, lanes(c)]), cap)
            bar = 2.0 * new - old
            flow_out[:, lanes(c)] = new
            s_b[k, c] = bar
            k_b.append(send(s_b.at[k, c], x_b.at[k, c], b_s.at[k, c], b_r.at[k, c], t, qn))
            bars[c, F0 : F0 + cuts, :] = split(bar)

        def cut_in(k, c):
            k_b[k * chunks + c].wait_recv()
            bars[c, T0 : T0 + cuts, :] = split(x_b[k, c])

        def plant_prices(c, value):
            return joined(dot(inc[P0 : P0 + pad, :], value))[:plants]

        def release_step(c, price, old_ref, dual_ref, out_ref):
            old = old_ref[:, lanes(c)]
            new = jnp.maximum(0.0, old + PRIMAL * (price + dual_ref[:, lanes(c)]))
            bar = 2.0 * new - old
            out_ref[:, lanes(c)] = new
            padr[0:plants, :] = bar
            bars[c, P0 : P0 + pad, :] = split(padr[...])
            return bar

        def gen_step(c, old_ref, price_ref, dual_ref, out_ref):
            cost = colf[c_gen : c_gen + buses, :]
            old = old_ref[:, lanes(c)]
            new = jnp.maximum(
                0.0, old - PRIMAL * (cost - price_ref[:, lanes(c)] + dual_ref[:, lanes(c)])
            )
            gbar[:, lanes(c)] = 2.0 * new - old
            out_ref[:, lanes(c)] = new

        lane = lax.broadcasted_iota(jnp.int32, (plants, W), 1)

        def level_step(k, dual_ref, old_ref, out_ref):
            cap = colf[c_sto : c_sto + pad, :][:plants]
            rolled = [pltpu.roll(dual_ref[:, lanes(c)], W - 1, 1) for c in range(chunks)]
            rolled.append(pltpu.roll(x_ds[k], W - 1, 1))
            for c in range(chunks):
                after = jnp.where(lane == W - 1, rolled[c + 1], rolled[c])
                old = old_ref[:, lanes(c)]
                new = jnp.minimum(
                    jnp.maximum(old + PRIMAL * (dual_ref[:, lanes(c)] - after), 0.0), cap
                )
                lbar[k, :, lanes(c)] = 2.0 * new - old
                out_ref[:, lanes(c)] = new
            return send(
                lbar.at[k, :, pl.ds(hours - W, W)], x_lb.at[k], lb_s.at[k], lb_r.at[k], tn, q
            )

        def storage_step(k, dual_ref, relbars, out_ref):
            rolled = [pltpu.roll(x_lb[k], 1, 1)]
            rolled += [pltpu.roll(lbar[k, :, lanes(c)], 1, 1) for c in range(chunks)]
            for c in range(chunks):
                before = jnp.where(lane == 0, rolled[c], rolled[c + 1])
                inflow = own[c][:plants]
                out_ref[:, lanes(c)] = dual_ref[:, lanes(c)] + DUAL * (
                    inflow - lbar[k, :, lanes(c)] + before - relbars(c)
                )

        def balance_step(c, old_ref, out_ref):
            balance = gbar[:, lanes(c)] + joined(dot(inct[...], bars[c]))
            out_ref[:, lanes(c)] = old_ref[:, lanes(c)] + DUAL * (dem[:, lanes(c)] - balance)

        def cap_dual_step(cap_bar, dual_ref, out_ref):
            col = columns(cap_bar)
            for c in range(chunks):
                out_ref[:, lanes(c)] = jnp.maximum(
                    0.0,
                    dual_ref[:, lanes(c)] - DUAL * (av[:, lanes(c)] * col - gbar[:, lanes(c)]),
                )

        for c in range(chunks):
            line_step(c, split(bal[:, lanes(c)]), lf, o_lf)
        for c in range(chunks):
            cut_step(0, c, cf, o_cf)
        for c in range(chunks):
            release_step(c, plant_prices(c, split(bal[:, lanes(c)])), rel, ds, o_rel)

        terms(mate, near)
        k_inf = []
        for c in range(chunks):
            k_far[c].wait_recv()
            near[c, 0:srow, :] = near[c, 0:srow, :] + x_far[c]
            k_inf.append(
                send(near.at[c, pl.ds(0, srow)], x_inf.at[c], inf_s.at[c], inf_r.at[c], t, mate)
            )

        loads["gen"].wait()
        for c in range(chunks):
            gen_step(c, gen, bal, dc, o_gen)
        loads["lev"].wait()
        k_ds[0].wait_recv()
        k_lb = [level_step(0, ds, lev, o_lev)]

        cost = floats[:, r_cost : r_cost + buses]
        cap_old = floats[:, r_cap : r_cap + buses]
        cap_one = jnp.maximum(0.0, cap_old - cap_step * (cost - price_all(0)))
        cap_dual_step(2.0 * cap_one - cap_old, dc, o_dc)
        price_out(1, lambda c: o_dc[:, lanes(c)])

        terms(q, own)

        loads["dem"].wait()
        for c in range(chunks):
            cut_in(0, c)
            balance_step(c, bal, o_bal)
            send_prices(1, c, split(o_bal[:, lanes(c)]))

        for c in range(chunks):
            line_step(c, split(o_bal[:, lanes(c)]), o_lf, o_lf)
        for c in range(chunks):
            cut_step(1, c, o_cf, o_cf)
        for c in range(chunks):
            k_inf[c].wait_recv()
            own[c, 0:srow, :] = own[c, 0:srow, :] + x_inf[c]
        k_lb[0].wait_recv()
        storage_step(0, ds, lambda c: 2.0 * o_rel[:, lanes(c)] - rel[:, lanes(c)], o_ds)
        k_ds.append(send(o_ds.at[:, pl.ds(0, W)], x_ds.at[1], ds_s.at[1], ds_r.at[1], tp, q))
        relbar = [
            release_step(c, plant_prices(c, split(o_bal[:, lanes(c)])), o_rel, o_ds, o_rel)
            for c in range(chunks)
        ]
        for c in range(chunks):
            gen_step(c, o_gen, o_bal, o_dc, o_gen)
        cap_two = jnp.maximum(0.0, cap_one - cap_step * (cost - price_all(1)))
        o_cap[...] = cap_two
        cap_dual_step(2.0 * cap_two - cap_one, o_dc, o_dc)
        k_ds[1].wait_recv()
        k_lb.append(level_step(1, o_ds, o_lev, o_lev))
        k_lb[1].wait_recv()
        k_ds[1].wait_send()
        storage_step(1, o_ds, lambda c: relbar[c], o_ds)
        for c in range(chunks):
            cut_in(1, c)
            balance_step(c, o_bal, o_bal)
        for copy in sent:
            if copy is not k_ds[1]:
                copy.wait_send()

    def big(n, kind=F32):
        return pltpu.VMEM((n, hours), kind)

    dma = pltpu.SemaphoreType.DMA
    scratch = [
        big(buses), big(buses), big(cells, BF16), big(buses), big(plants), big(plants),
        big(lines), big(cuts), big(buses), big(buses), big(plants),
        pltpu.VMEM((rows, buses), BF16),
        pltpu.VMEM((buses, rows), BF16),
        pltpu.VMEM((chunks, rows, 2 * W), BF16),
        big(buses),
        pltpu.VMEM((2, plants, hours), F32),
        pltpu.VMEM((r_cost, W), F32),
        pltpu.VMEM((pad, W), F32),
        big(cuts),
        pltpu.VMEM((chunks, prow, W), F32),
        pltpu.VMEM((chunks, prow, W), F32),
        pltpu.VMEM((chunks, prow, W), F32),
        pltpu.VMEM((1, cuts), jnp.int32),
        pltpu.VMEM((2, plants, W), F32),
        pltpu.VMEM((2, plants, W), F32),
        pltpu.VMEM((2, chunks, cuts, W), F32),
        pltpu.VMEM((2, chunks, cuts, W), F32),
        pltpu.VMEM((2, chunks, cuts, W), F32),
        pltpu.VMEM((2, chunks, cuts, W), F32),
        pltpu.VMEM((chunks, srow, W), F32),
        pltpu.VMEM((chunks, srow, W), F32),
        pltpu.VMEM((2, times, 1, buses), F32),
        dma((10 + parts,)),
        dma, dma, dma((2,)), dma((2,)), dma((2,)), dma((2,)),
        dma((2, chunks)), dma((2, chunks)), dma((2, chunks)), dma((2, chunks)),
        dma((chunks,)), dma((chunks,)), dma((chunks,)), dma((chunks,)),
        dma((2,)), dma((2,)),
    ]
    return kernel, scratch, pad


def solution(mesh):
    times, zones = mesh.shape["tm"], mesh.shape["net"]

    def local(
        demand, availability, gen_cost, cap_cost, runoff, cell_plant, plant_bus, store_cap,
        line_from, line_to, line_cap, cut_from, cut_to, cut_cap, generation, capacity,
        release, storage_level, line_flow, cut_flow, dual_bal, dual_cap, dual_sto,
    ):
        buses, hours = demand.shape
        plants, lines, cuts, cells = (
            release.shape[0], line_flow.shape[0], cut_flow.shape[0], runoff.shape[0],
        )
        kernel, scratch, pad = make_kernel((buses, plants, lines, cuts, cells, hours, times, zones))
        more = pad - plants
        ints = jnp.concatenate(
            [line_to, line_from, cut_from, cut_to, jnp.pad(plant_bus, (0, more), constant_values=-1)]
        ).reshape(1, -1)
        floats = jnp.concatenate(
            [gen_cost, line_cap, cut_cap, jnp.pad(store_cap, (0, more)), cap_cost, capacity]
        ).reshape(1, -1)
        vmem = pl.BlockSpec(memory_space=pltpu.VMEM)
        hbm = pl.BlockSpec(memory_space=pl.ANY)

        def shape(n):
            return jax.ShapeDtypeStruct((n, hours), F32)

        outs = pl.pallas_call(
            kernel,
            out_shape=(
                shape(buses), jax.ShapeDtypeStruct((1, buses), F32), shape(plants), shape(plants),
                shape(lines), shape(cuts), shape(buses), shape(buses), shape(plants),
            ),
            in_specs=[vmem] * 3 + [hbm] * 11,
            out_specs=(vmem,) * 9,
            scratch_shapes=scratch,
            compiler_params=pltpu.CompilerParams(
                collective_id=0, has_side_effects=True, vmem_limit_bytes=48 << 20
            ),
        )(
            ints, floats, cell_plant.reshape(1, -1),
            demand, availability, runoff, generation, release, storage_level, line_flow, cut_flow,
            dual_bal, dual_cap, dual_sto,
        )
        outs = list(outs)
        outs[1] = outs[1].reshape(buses)
        return tuple(outs)

    both, net = P("net", "tm"), P("net")
    in_specs = (both, both, net, net, both) + (net,) * 9 + (both, net) + (both,) * 7
    out_specs = (both, net) + (both,) * 7
    return jax.shard_map(local, mesh=mesh, in_specs=in_specs, out_specs=out_specs, check_vma=False)
```

```python
import jax
import jax.numpy as jnp
from jax import lax
from jax.experimental import pallas as pl
from jax.experimental.pallas import tpu as pltpu
from jax.sharding import PartitionSpec as P

MESH = pl.DeviceIdType.MESH
PRIMAL = 0.4
DUAL = 0.4
W = 128
F32 = jnp.float32
BF16 = jnp.bfloat16


def split(values):
    hi = values.astype(BF16)
    lo = (values - hi.astype(F32)).astype(BF16)
    return jnp.concatenate([hi, lo], axis=1)


def joined(product):
    return product[:, :W] + product[:, W:]


def dot(a, b):
    return jnp.dot(a, b, preferred_element_type=F32)


def columns(row):
    blocks = []
    for i in range(row.shape[1] // W):
        blocks.append(jnp.transpose(jnp.broadcast_to(row[:, i * W : (i + 1) * W], (W, W))))
    return jnp.concatenate(blocks, axis=0) if len(blocks) > 1 else blocks[0]


def wide(block, count):
    return jnp.concatenate([block] * count, axis=1) if count > 1 else block


def make_kernel(sizes):
    buses, plants, lines, cuts, cells, hours, times, zones = sizes
    chunks = hours // W
    pad = -(-plants // W) * W
    prow = -(-plants // 16) * 16
    srow = -(-plants // 8) * 8
    parts = 4
    depth = cells // parts
    L0, F0, P0 = 0, lines, lines + cuts
    T0 = P0 + pad
    rows = T0 + cuts
    mid = times // 4
    c_gen, c_line, c_cut, c_sto = 0, buses, buses + lines, buses + lines + cuts
    c_rows = c_sto + pad
    cap_step = PRIMAL / (hours * times)

    def kernel(
        h_cell, h_pl, h_sto, h_to, h_from, h_lcap, h_cfrom, h_cto, h_ccap, h_gcost, h_ccost, h_cap,
        h_dem, h_av, h_run, h_gen, h_rel, h_lev, h_lf, h_cf, h_bal, h_dc, h_ds,
        o_gen, o_cap, o_rel, o_lev, o_lf, o_cf, o_bal, o_dc, o_ds,
        cell, r_pl, r_sto, r_to, r_from, r_lcap, r_cfrom, r_cto, r_ccap, r_gcost, r_ccost, r_cap,
        dem, av, run, gen, rel, lev, lf, cf, bal, dc, ds,
        inc, inct, bars, gbar, lbar, colf, padr, p_pl, p_sto, dcut, far, near, own,
        x_ct, x_ds, x_lb, s_p, x_p, s_b, x_b, x_far, x_inf, slot_a, slot_b,
        isem, ct_s, ct_r, ds_s, ds_r, lb_s, lb_r, p_s, p_r, b_s, b_r, far_s, far_r, inf_s, inf_r, pa_s, pa_r, pb_s, pb_r,
    ):
        t = lax.axis_index("tm")
        q = lax.axis_index("net")
        qn = lax.rem(q + 1, zones)
        qp = lax.rem(q + zones - 1, zones)
        sign = 1 - 2 * lax.rem(q, 2)
        mate = q + sign
        far_zone = lax.rem(q - sign + zones, zones)
        far_to = lax.rem(q - 2 * sign + zones, zones)
        tn = lax.rem(t + 1, times)
        tp = lax.rem(t + times - 1, times)

        loads = {}
        pairs = [
            ("cell", h_cell, cell), ("cto", h_cto, r_cto), ("to", h_to, r_to),
            ("from", h_from, r_from), ("cfrom", h_cfrom, r_cfrom), ("pl", h_pl, r_pl),
            ("gcost", h_gcost, r_gcost), ("lcap", h_lcap, r_lcap), ("ccap", h_ccap, r_ccap),
            ("sto", h_sto, r_sto), ("ccost", h_ccost, r_ccost), ("cap", h_cap, r_cap),
            ("av", h_av, av), ("dc", h_dc, dc),
        ]
        for k in range(parts):
            at = pl.ds(k * depth, depth)
            pairs.append((("run", k), h_run.at[at], run.at[at]))
        pairs += [
            ("ds", h_ds, ds), ("bal", h_bal, bal), ("lf", h_lf, lf), ("cf", h_cf, cf),
            ("gen", h_gen, gen), ("rel", h_rel, rel), ("lev", h_lev, lev), ("dem", h_dem, dem),
        ]
        for n, (name, src, dst) in enumerate(pairs):
            loads[name] = pltpu.make_async_copy(src, dst, isem.at[n])
            loads[name].start()

        barrier = pltpu.get_barrier_semaphore()

        core = lax.rem(t, 2)
        z = lax.rem(t // 2, mid)
        y = t // (2 * mid)

        def square(i):
            return ((1 - y if i // 2 else y) * mid + z) * 2 + (1 - core if i % 2 else core)

        def along(i):
            return (y * mid + lax.rem(z + i, mid)) * 2 + core

        def greet(tt, qq):
            pl.semaphore_signal(barrier, inc=1, device_id=(tt, qq), device_id_type=MESH)

        for d in (1, 2, zones - 2, zones - 1):
            greet(t, lax.rem(q + d, zones))
        for i in range(1, 4):
            greet(square(i), q)
        greet(lax.rem(t + 2 * core - 1 + times, times), q)
        for i in range(1, mid):
            greet(along(i), q)

        sent = []

        def send(src, dst, ssem, rsem, tt, qq):
            copy = pltpu.make_async_remote_copy(
                src_ref=src, dst_ref=dst, send_sem=ssem, recv_sem=rsem,
                device_id=(tt, qq), device_id_type=MESH,
            )
            copy.start()
            sent.append(copy)
            return copy

        def lanes(c):
            return slice(c * W, (c + 1) * W)

        def price_row(dual_of):
            total = None
            for c in range(chunks):
                term = av[:, lanes(c)] * dual_of(c)
                total = term if total is None else total + term
            return jnp.concatenate(
                [
                    jnp.sum(jnp.transpose(total[i * W : (i + 1) * W]), axis=0, keepdims=True)
                    for i in range(buses // W)
                ],
                axis=1,
            )

        def price_copy(slot, k, i, ssem, rsem, tt):
            return pltpu.make_async_remote_copy(
                src_ref=slot.at[k, 0], dst_ref=slot.at[k, i], send_sem=ssem.at[k],
                recv_sem=rsem.at[k], device_id=(tt, q), device_id_type=MESH,
            )

        def price_wait(slot, k, count, ssem, rsem, tt):
            everyone = slot.at[k, pl.ds(1, count - 1)]
            whole = pltpu.make_async_remote_copy(
                src_ref=everyone, dst_ref=everyone, send_sem=ssem.at[k], recv_sem=rsem.at[k],
                device_id=(tt, q), device_id_type=MESH,
            )
            whole.wait_recv()
            whole.wait_send()

        def price_first(k, row):
            slot_a[k, 0] = row
            for i in range(1, 4):
                price_copy(slot_a, k, i, pa_s, pa_r, square(i)).start()

        def price_second(k):
            price_wait(slot_a, k, 4, pa_s, pa_r, square(1))
            total = None
            for yy in (0, 1):
                for cc in (0, 1):
                    term = slot_a[k, (1 - y if yy else y) * 2 + (1 - core if cc else core)]
                    total = term if total is None else total + term
            slot_b[k, 0] = total
            for i in range(1, mid):
                price_copy(slot_b, k, i, pb_s, pb_r, along(i)).start()

        def price_all(k):
            price_wait(slot_b, k, mid, pb_s, pb_r, along(1))
            total = slot_b[k, lax.rem(z + mid, mid)]
            for j in range(1, mid):
                total = total + slot_b[k, lax.rem(z - j + mid, mid)]
            return total

        lane_bus = lax.broadcasted_iota(jnp.int32, (W, buses), 1)
        row_bus = lax.broadcasted_iota(jnp.int32, (buses, W), 0)
        one, zero = F32(1.0), F32(0.0)

        def flags(mask):
            return jnp.where(mask, one, zero)

        def place(at, to_row, from_row):
            m = jnp.zeros((W, buses), F32)
            mt = jnp.zeros((buses, W), F32)
            if to_row is not None:
                m = m + flags(wide(columns(to_row), buses // W) == lane_bus)
                mt = mt + flags(to_row == row_bus)
            if from_row is not None:
                m = m - flags(wide(columns(from_row), buses // W) == lane_bus)
                mt = mt - flags(from_row == row_bus)
            inc[at : at + W, :] = m.astype(BF16)
            inct[:, at : at + W] = mt.astype(BF16)

        for name in ("cto", "to", "from", "cfrom", "pl", "gcost", "lcap", "ccap", "sto", "ccost", "cap", "cell"):
            loads[name].wait()
        p_pl[...] = jnp.full_like(p_pl, -1)
        p_pl[:, 0:plants] = r_pl[...]
        p_sto[...] = jnp.zeros_like(p_sto)
        p_sto[:, 0:plants] = r_sto[...]
        for i in range(lines // W):
            place(L0 + i * W, r_to[i : i + 1, :], r_from[i : i + 1, :])
            colf[c_line + i * W : c_line + (i + 1) * W, :] = columns(r_lcap[i : i + 1, :])
        for i in range(cuts // W):
            place(F0 + i * W, None, r_cfrom[:, i * W : (i + 1) * W])
        for i in range(pad // W):
            place(P0 + i * W, p_pl[:, i * W : (i + 1) * W], None)
        for at, row in ((c_gen, r_gcost), (c_cut, r_ccap), (c_sto, p_sto)):
            colf[at : at + row.shape[1], :] = columns(row[...])
        padr[...] = jnp.zeros_like(padr)

        k_p, k_b = [], []

        def send_prices(k, c, value):
            s_p[k, c] = joined(dot(inc[T0:rows, :], value))
            k_p.append(send(s_p.at[k, c], x_p.at[k, c], p_s.at[k, c], p_r.at[k, c], t, qp))

        def terms(zone, out):
            ids = lax.broadcasted_iota(jnp.int32, (prow, depth), 0) + zone * plants
            total = None
            for k in range(parts):
                if ("run", k) in loads:
                    loads.pop(("run", k)).wait()
                onehot = flags(ids == cell[:, k * depth : (k + 1) * depth]).astype(BF16)
                term = dot(onehot, run[k * depth : (k + 1) * depth, :])
                total = term if total is None else total + term
            for c in range(chunks):
                out[c] = total[:, lanes(c)]

        loads["av"].wait()
        loads["dc"].wait()
        row = price_row(lambda c: dc[:, lanes(c)])
        terms(far_zone, far)
        loads["ds"].wait()

        pl.semaphore_wait(barrier, mid + 7)
        k_ct = send(r_cto, x_ct, ct_s, ct_r, t, qn)
        k_far = [
            send(far.at[c, pl.ds(0, srow)], x_far.at[c], far_s.at[c], far_r.at[c], t, far_to)
            for c in range(chunks)
        ]
        k_ds = [send(ds.at[:, pl.ds(0, W)], x_ds.at[0], ds_s.at[0], ds_r.at[0], tp, q)]
        price_first(0, row)
        terms(mate, near)

        k_ct.wait_recv()
        for i in range(cuts // W):
            place(T0 + i * W, x_ct[:, i * W : (i + 1) * W], None)
        loads["bal"].wait()
        for c in range(chunks):
            send_prices(0, c, split(bal[:, lanes(c)]))

        def bound(v, b):
            return jnp.minimum(jnp.maximum(v, -b), b)

        def line_step(c, value, flow, flow_out):
            diff = joined(dot(inc[L0:P0, :], value))
            cap = colf[c_line : c_line + lines, :]
            old = flow[:, lanes(c)]
            new = bound(old + PRIMAL * diff[:lines], cap)
            bars[c, L0 : L0 + lines, :] = split(2.0 * new - old)
            flow_out[:, lanes(c)] = new
            dcut[:, lanes(c)] = diff[lines:]

        def cut_step(k, c, flow, flow_out):
            k_p[k * chunks + c].wait_recv()
            cap = colf[c_cut : c_cut + cuts, :]
            old = flow[:, lanes(c)]
            new = bound(old + PRIMAL * (x_p[k, c] + dcut[:, lanes(c)]), cap)
            bar = 2.0 * new - old
            flow_out[:, lanes(c)] = new
            s_b[k, c] = bar
            k_b.append(send(s_b.at[k, c], x_b.at[k, c], b_s.at[k, c], b_r.at[k, c], t, qn))
            bars[c, F0 : F0 + cuts, :] = split(bar)

        def cut_in(k, c, out_ref):
            k_b[k * chunks + c].wait_recv()
            more = joined(dot(inct[:, T0:rows], split(x_b[k, c])))
            out_ref[:, lanes(c)] = out_ref[:, lanes(c)] - DUAL * more

        def plant_prices(c, value):
            return joined(dot(inc[P0 : P0 + pad, :], value))[:plants]

        def release_step(c, price, old_ref, dual_ref, out_ref):
            old = old_ref[:, lanes(c)]
            new = jnp.maximum(0.0, old + PRIMAL * (price + dual_ref[:, lanes(c)]))
            bar = 2.0 * new - old
            out_ref[:, lanes(c)] = new
            padr[0:plants, :] = bar
            bars[c, P0 : P0 + pad, :] = split(padr[...])
            return bar

        def gen_step(c, old_ref, price_ref, dual_ref, out_ref):
            cost = colf[c_gen : c_gen + buses, :]
            old = old_ref[:, lanes(c)]
            new = jnp.maximum(
                0.0, old - PRIMAL * (cost - price_ref[:, lanes(c)] + dual_ref[:, lanes(c)])
            )
            gbar[:, lanes(c)] = 2.0 * new - old
            out_ref[:, lanes(c)] = new

        lane = lax.broadcasted_iota(jnp.int32, (plants, W), 1)

        def level_step(k, dual_ref, old_ref, out_ref):
            cap = colf[c_sto : c_sto + pad, :][:plants]
            rolled = [pltpu.roll(dual_ref[:, lanes(c)], W - 1, 1) for c in range(chunks)]
            rolled.append(pltpu.roll(x_ds[k], W - 1, 1))
            for c in range(chunks):
                after = jnp.where(lane == W - 1, rolled[c + 1], rolled[c])
                old = old_ref[:, lanes(c)]
                new = jnp.minimum(
                    jnp.maximum(old + PRIMAL * (dual_ref[:, lanes(c)] - after), 0.0), cap
                )
                lbar[k, :, lanes(c)] = 2.0 * new - old
                out_ref[:, lanes(c)] = new
            return send(
                lbar.at[k, :, pl.ds(hours - W, W)], x_lb.at[k], lb_s.at[k], lb_r.at[k], tn, q
            )

        def storage_step(k, dual_ref, relbars, out_ref):
            rolled = [pltpu.roll(x_lb[k], 1, 1)]
            rolled += [pltpu.roll(lbar[k, :, lanes(c)], 1, 1) for c in range(chunks)]
            for c in range(chunks):
                before = jnp.where(lane == 0, rolled[c], rolled[c + 1])
                inflow = own[c][:plants]
                out_ref[:, lanes(c)] = dual_ref[:, lanes(c)] + DUAL * (
                    inflow - lbar[k, :, lanes(c)] + before - relbars(c)
                )

        def balance_step(c, old_ref, out_ref):
            balance = gbar[:, lanes(c)] + joined(dot(inct[:, 0:T0], bars[c]))
            out_ref[:, lanes(c)] = old_ref[:, lanes(c)] + DUAL * (dem[:, lanes(c)] - balance)

        def cap_dual_step(cap_bar, dual_ref, out_ref):
            col = columns(cap_bar)
            for c in range(chunks):
                out_ref[:, lanes(c)] = jnp.maximum(
                    0.0,
                    dual_ref[:, lanes(c)] - DUAL * (av[:, lanes(c)] * col - gbar[:, lanes(c)]),
                )

        def send_inflow(c):
            k_far[c].wait_recv()
            near[c, 0:srow, :] = near[c, 0:srow, :] + x_far[c]
            k_inf.append(
                send(near.at[c, pl.ds(0, srow)], x_inf.at[c], inf_s.at[c], inf_r.at[c], t, mate)
            )

        k_inf = []
        loads["lf"].wait()
        for c in range(chunks):
            line_step(c, split(bal[:, lanes(c)]), lf, o_lf)
        loads["cf"].wait()
        cut_step(0, 0, cf, o_cf)
        loads["gen"].wait()
        for c in range(chunks):
            gen_step(c, gen, bal, dc, o_gen)
        send_inflow(0)
        cut_step(0, 1, cf, o_cf)
        price_second(0)
        loads["rel"].wait()
        for c in range(chunks):
            release_step(c, plant_prices(c, split(bal[:, lanes(c)])), rel, ds, o_rel)
        send_inflow(1)
        cut_step(0, 2, cf, o_cf)
        loads["dem"].wait()
        for c in range(chunks):
            balance_step(c, bal, o_bal)
            cut_in(0, c, o_bal)
            send_prices(1, c, split(o_bal[:, lanes(c)]))
        send_inflow(2)

        loads["lev"].wait()
        k_ds[0].wait_recv()
        k_lb = [level_step(0, ds, lev, o_lev)]
        cost = r_ccost[...]
        cap_old = r_cap[...]
        cap_one = jnp.maximum(0.0, cap_old - cap_step * (cost - price_all(0)))
        cap_dual_step(2.0 * cap_one - cap_old, dc, o_dc)
        price_first(1, price_row(lambda c: o_dc[:, lanes(c)]))

        for c in range(chunks):
            line_step(c, split(o_bal[:, lanes(c)]), o_lf, o_lf)
            cut_step(1, c, o_cf, o_cf)
        price_second(1)
        for c in range(chunks):
            gen_step(c, o_gen, o_bal, o_dc, o_gen)
        terms(q, own)
        for c in range(chunks):
            k_inf[c].wait_recv()
            own[c, 0:srow, :] = own[c, 0:srow, :] + x_inf[c]
        k_lb[0].wait_recv()
        storage_step(0, ds, lambda c: 2.0 * o_rel[:, lanes(c)] - rel[:, lanes(c)], o_ds)
        k_ds.append(send(o_ds.at[:, pl.ds(0, W)], x_ds.at[1], ds_s.at[1], ds_r.at[1], tp, q))
        relbar = [
            release_step(c, plant_prices(c, split(o_bal[:, lanes(c)])), o_rel, o_ds, o_rel)
            for c in range(chunks)
        ]
        k_ds[1].wait_recv()
        k_lb.append(level_step(1, o_ds, o_lev, o_lev))
        for c in range(chunks):
            balance_step(c, o_bal, o_bal)
        cap_two = jnp.maximum(0.0, cap_one - cap_step * (cost - price_all(1)))
        o_cap[...] = cap_two
        cap_dual_step(2.0 * cap_two - cap_one, o_dc, o_dc)
        for c in range(chunks):
            cut_in(1, c, o_bal)
        k_lb[1].wait_recv()
        k_ds[1].wait_send()
        storage_step(1, o_ds, lambda c: relbar[c], o_ds)
        for copy in sent:
            if copy is not k_ds[1]:
                copy.wait_send()

    def big(n, kind=F32):
        return pltpu.VMEM((n, hours), kind)

    dma = pltpu.SemaphoreType.DMA
    def row(n, kind=F32):
        return pltpu.VMEM((1, n), kind)

    def lrow(kind):
        return pltpu.VMEM((lines // W, W), kind)

    i32 = jnp.int32
    scratch = [
        row(cells, i32), row(plants, i32), row(plants), lrow(i32), lrow(i32), lrow(F32),
        row(cuts, i32), row(cuts, i32), row(cuts), row(buses), row(buses), row(buses),
        big(buses), big(buses), big(cells, BF16), big(buses), big(plants), big(plants),
        big(lines), big(cuts), big(buses), big(buses), big(plants),
        pltpu.VMEM((rows, buses), BF16),
        pltpu.VMEM((buses, rows), BF16),
        pltpu.VMEM((chunks, rows - cuts, 2 * W), BF16),
        big(buses),
        pltpu.VMEM((2, plants, hours), F32),
        pltpu.VMEM((c_rows, W), F32),
        pltpu.VMEM((pad, W), F32),
        row(pad, i32), row(pad),
        big(cuts),
        pltpu.VMEM((chunks, prow, W), F32),
        pltpu.VMEM((chunks, prow, W), F32),
        pltpu.VMEM((chunks, prow, W), F32),
        pltpu.VMEM((1, cuts), jnp.int32),
        pltpu.VMEM((2, plants, W), F32),
        pltpu.VMEM((2, plants, W), F32),
        pltpu.VMEM((2, chunks, cuts, W), F32),
        pltpu.VMEM((2, chunks, cuts, W), F32),
        pltpu.VMEM((2, chunks, cuts, W), F32),
        pltpu.VMEM((2, chunks, cuts, W), F32),
        pltpu.VMEM((chunks, srow, W), F32),
        pltpu.VMEM((chunks, srow, W), F32),
        pltpu.VMEM((2, 4, 1, buses), F32),
        pltpu.VMEM((2, mid, 1, buses), F32),
        dma((22 + parts,)),
        dma, dma, dma((2,)), dma((2,)), dma((2,)), dma((2,)),
        dma((2, chunks)), dma((2, chunks)), dma((2, chunks)), dma((2, chunks)),
        dma((chunks,)), dma((chunks,)), dma((chunks,)), dma((chunks,)),
        dma((2,)), dma((2,)), dma((2,)), dma((2,)),
    ]
    return kernel, scratch


def write_out(*refs):
    count = len(refs) // 2
    sem = refs[-1]
    copies = [
        pltpu.make_async_copy(refs[i], refs[count + i], sem.at[i]) for i in range(count)
    ]
    for copy in copies:
        copy.start()
    for copy in copies:
        copy.wait()


def solution(mesh):
    times, zones = mesh.shape["tm"], mesh.shape["net"]

    def local(
        demand, availability, gen_cost, cap_cost, runoff, cell_plant, plant_bus, store_cap,
        line_from, line_to, line_cap, cut_from, cut_to, cut_cap, generation, capacity,
        release, storage_level, line_flow, cut_flow, dual_bal, dual_cap, dual_sto,
    ):
        buses, hours = demand.shape
        plants, lines, cuts, cells = (
            release.shape[0], line_flow.shape[0], cut_flow.shape[0], runoff.shape[0],
        )
        kernel, scratch = make_kernel((buses, plants, lines, cuts, cells, hours, times, zones))
        hbm = pl.BlockSpec(memory_space=pltpu.HBM)
        shapes = [(n, hours) for n in (buses, 0, plants, plants, lines, cuts, buses, buses, plants)]
        shapes[1] = (1, buses)

        def row(values):
            return values.reshape(1, -1)

        def tiles(values):
            return values.reshape(-1, W)

        outs = pl.pallas_call(
            kernel,
            out_shape=tuple(pltpu.VMEM(shape, F32) for shape in shapes),
            in_specs=[hbm] * 23,
            out_specs=(pl.BlockSpec(memory_space=pltpu.VMEM),) * 9,
            scratch_shapes=scratch,
            compiler_params=pltpu.CompilerParams(
                collective_id=0, has_side_effects=True, vmem_limit_bytes=59 << 20
            ),
        )(
            row(cell_plant), row(plant_bus), row(store_cap), tiles(line_to), tiles(line_from),
            tiles(line_cap), row(cut_from), row(cut_to), row(cut_cap), row(gen_cost), row(cap_cost),
            row(capacity),
            demand, availability, runoff, generation, release, storage_level, line_flow, cut_flow,
            dual_bal, dual_cap, dual_sto,
        )
        outs = pl.pallas_call(
            write_out,
            out_shape=tuple(jax.ShapeDtypeStruct(shape, F32) for shape in shapes),
            in_specs=[pl.BlockSpec(memory_space=pl.ANY)] * 9,
            out_specs=(hbm,) * 9,
            scratch_shapes=[pltpu.SemaphoreType.DMA((9,))],
            compiler_params=pltpu.CompilerParams(vmem_limit_bytes=1 << 20),
        )(*outs)
        outs = list(outs)
        outs[1] = outs[1].reshape(buses)
        return tuple(outs)

    both, net = P("net", "tm"), P("net")
    in_specs = (both, both, net, net, both) + (net,) * 9 + (both, net) + (both,) * 7
    out_specs = (both, net) + (both,) * 7
    return jax.shard_map(local, mesh=mesh, in_specs=in_specs, out_specs=out_specs, check_vma=False)
```

```python
import jax
import jax.numpy as jnp
from jax import lax
from jax.experimental import pallas as pl
from jax.experimental.pallas import tpu as pltpu
from jax.sharding import PartitionSpec as P

MESH = pl.DeviceIdType.MESH
PRIMAL = 0.4
DUAL = 0.4
W = 128
F32 = jnp.float32
BF16 = jnp.bfloat16


def split(values):
    hi = values.astype(BF16)
    lo = (values - hi.astype(F32)).astype(BF16)
    return jnp.concatenate([hi, lo], axis=1)


def joined(product):
    return product[:, :W] + product[:, W:]


def dot(a, b):
    return jnp.dot(a, b, preferred_element_type=F32)


def columns(row):
    blocks = []
    for i in range(row.shape[1] // W):
        blocks.append(jnp.transpose(jnp.broadcast_to(row[:, i * W : (i + 1) * W], (W, W))))
    return jnp.concatenate(blocks, axis=0) if len(blocks) > 1 else blocks[0]


def wide(block, count):
    return jnp.concatenate([block] * count, axis=1) if count > 1 else block


def make_kernel(sizes):
    buses, plants, lines, cuts, cells, hours, times, zones = sizes
    chunks = hours // W
    pad = -(-plants // W) * W
    prow = -(-plants // 16) * 16
    srow = -(-plants // 8) * 8
    parts = 4
    depth = cells // parts
    L0, F0, P0 = 0, lines, lines + cuts
    T0 = P0 + pad
    rows = T0 + cuts
    mid = times // 4
    c_gen, c_line, c_cut, c_sto = 0, buses, buses + lines, buses + lines + cuts
    c_rows = c_sto + pad
    cap_step = PRIMAL / (hours * times)

    def kernel(
        h_cell, h_pl, h_sto, h_to, h_from, h_lcap, h_cfrom, h_cto, h_ccap, h_gcost, h_ccost, h_cap,
        h_dem, h_av, h_run, h_gen, h_rel, h_lev, h_lf, h_cf, h_bal, h_dc, h_ds,
        o_gen, o_cap, o_rel, o_lev, o_lf, o_cf, o_bal, o_dc, o_ds,
        cell, r_pl, r_sto, r_to, r_from, r_lcap, r_cfrom, r_cto, r_ccap, r_gcost, r_ccost, r_cap,
        dem, av, run, gen, rel, lev, lf, cf, bal, dc, ds,
        inc, inct, bars, gbar, lbar, colf, padr, p_pl, p_sto, dcut, far, near, own,
        x_ct, x_ds, x_lb, s_p, x_p, s_b, x_b, x_far, x_inf, slot_a, slot_b,
        isem, ct_s, ct_r, ds_s, ds_r, lb_s, lb_r, p_s, p_r, b_s, b_r, far_s, far_r, inf_s, inf_r, pa_s, pa_r, pb_s, pb_r,
    ):
        t = lax.axis_index("tm")
        q = lax.axis_index("net")
        qn = lax.rem(q + 1, zones)
        qp = lax.rem(q + zones - 1, zones)
        sign = 1 - 2 * lax.rem(q, 2)
        mate = q + sign
        far_zone = lax.rem(q - sign + zones, zones)
        far_to = lax.rem(q - 2 * sign + zones, zones)
        tn = lax.rem(t + 1, times)
        tp = lax.rem(t + times - 1, times)

        loads = {}
        pairs = [
            ("cell", h_cell, cell), ("cto", h_cto, r_cto), ("to", h_to, r_to),
            ("from", h_from, r_from), ("cfrom", h_cfrom, r_cfrom), ("pl", h_pl, r_pl),
            ("gcost", h_gcost, r_gcost), ("lcap", h_lcap, r_lcap), ("ccap", h_ccap, r_ccap),
            ("sto", h_sto, r_sto), ("ccost", h_ccost, r_ccost), ("cap", h_cap, r_cap),
            ("av", h_av, av), ("dc", h_dc, dc), ("ds", h_ds, ds), ("bal", h_bal, bal),
        ]
        for k in range(parts):
            at = pl.ds(k * depth, depth)
            pairs.append((("run", k), h_run.at[at], run.at[at]))
        pairs += [
            ("lf", h_lf, lf), ("cf", h_cf, cf),
            ("gen", h_gen, gen), ("rel", h_rel, rel), ("lev", h_lev, lev), ("dem", h_dem, dem),
        ]
        for n, (name, src, dst) in enumerate(pairs):
            loads[name] = pltpu.make_async_copy(src, dst, isem.at[n])
            loads[name].start()

        barrier = pltpu.get_barrier_semaphore()

        core = lax.rem(t, 2)
        z = lax.rem(t // 2, mid)
        y = t // (2 * mid)

        def square(i):
            return ((1 - y if i // 2 else y) * mid + z) * 2 + (1 - core if i % 2 else core)

        def along(i):
            return (y * mid + lax.rem(z + i, mid)) * 2 + core

        def greet(tt, qq):
            pl.semaphore_signal(barrier, inc=1, device_id=(tt, qq), device_id_type=MESH)

        for d in (1, 2, zones - 2, zones - 1):
            greet(t, lax.rem(q + d, zones))
        for i in range(1, 4):
            greet(square(i), q)
        greet(lax.rem(t + 2 * core - 1 + times, times), q)
        for i in range(1, mid):
            greet(along(i), q)

        sent = []

        def send(src, dst, ssem, rsem, tt, qq):
            copy = pltpu.make_async_remote_copy(
                src_ref=src, dst_ref=dst, send_sem=ssem, recv_sem=rsem,
                device_id=(tt, qq), device_id_type=MESH,
            )
            copy.start()
            sent.append(copy)
            return copy

        def lanes(c):
            return slice(c * W, (c + 1) * W)

        def price_row(dual_of):
            total = None
            for c in range(chunks):
                term = av[:, lanes(c)] * dual_of(c)
                total = term if total is None else total + term
            return jnp.concatenate(
                [
                    jnp.sum(jnp.transpose(total[i * W : (i + 1) * W]), axis=0, keepdims=True)
                    for i in range(buses // W)
                ],
                axis=1,
            )

        def price_copy(slot, k, i, ssem, rsem, tt):
            return pltpu.make_async_remote_copy(
                src_ref=slot.at[k, 0], dst_ref=slot.at[k, i], send_sem=ssem.at[k],
                recv_sem=rsem.at[k], device_id=(tt, q), device_id_type=MESH,
            )

        def price_wait(slot, k, count, ssem, rsem, tt):
            everyone = slot.at[k, pl.ds(1, count - 1)]
            whole = pltpu.make_async_remote_copy(
                src_ref=everyone, dst_ref=everyone, send_sem=ssem.at[k], recv_sem=rsem.at[k],
                device_id=(tt, q), device_id_type=MESH,
            )
            whole.wait_recv()
            whole.wait_send()

        def price_first(k, row):
            slot_a[k, 0] = row
            for i in range(1, 4):
                price_copy(slot_a, k, i, pa_s, pa_r, square(i)).start()

        def price_second(k):
            price_wait(slot_a, k, 4, pa_s, pa_r, square(1))
            total = None
            for yy in (0, 1):
                for cc in (0, 1):
                    term = slot_a[k, (1 - y if yy else y) * 2 + (1 - core if cc else core)]
                    total = term if total is None else total + term
            slot_b[k, 0] = total
            for i in range(1, mid):
                price_copy(slot_b, k, i, pb_s, pb_r, along(i)).start()

        def price_all(k):
            price_wait(slot_b, k, mid, pb_s, pb_r, along(1))
            total = slot_b[k, lax.rem(z + mid, mid)]
            for j in range(1, mid):
                total = total + slot_b[k, lax.rem(z - j + mid, mid)]
            return total

        lane_bus = lax.broadcasted_iota(jnp.int32, (W, buses), 1)
        row_bus = lax.broadcasted_iota(jnp.int32, (buses, W), 0)
        one, zero = F32(1.0), F32(0.0)

        def flags(mask):
            return jnp.where(mask, one, zero)

        def place(at, to_row, from_row):
            m = jnp.zeros((W, buses), F32)
            mt = jnp.zeros((buses, W), F32)
            if to_row is not None:
                m = m + flags(wide(columns(to_row), buses // W) == lane_bus)
                mt = mt + flags(to_row == row_bus)
            if from_row is not None:
                m = m - flags(wide(columns(from_row), buses // W) == lane_bus)
                mt = mt - flags(from_row == row_bus)
            inc[at : at + W, :] = m.astype(BF16)
            inct[:, at : at + W] = mt.astype(BF16)

        for name in ("cto", "to", "from", "cfrom", "pl", "gcost", "lcap", "ccap", "sto", "ccost", "cap", "cell"):
            loads[name].wait()
        p_pl[...] = jnp.full_like(p_pl, -1)
        p_pl[:, 0:plants] = r_pl[...]
        p_sto[...] = jnp.zeros_like(p_sto)
        p_sto[:, 0:plants] = r_sto[...]
        for i in range(lines // W):
            place(L0 + i * W, r_to[i : i + 1, :], r_from[i : i + 1, :])
            colf[c_line + i * W : c_line + (i + 1) * W, :] = columns(r_lcap[i : i + 1, :])
        for i in range(cuts // W):
            place(F0 + i * W, None, r_cfrom[:, i * W : (i + 1) * W])
        for i in range(pad // W):
            place(P0 + i * W, p_pl[:, i * W : (i + 1) * W], None)
        for at, row in ((c_gen, r_gcost), (c_cut, r_ccap), (c_sto, p_sto)):
            colf[at : at + row.shape[1], :] = columns(row[...])
        padr[...] = jnp.zeros_like(padr)

        k_p, k_b = [], []

        def send_prices(k, c, value):
            s_p[k, c] = joined(dot(inc[T0:rows, :], value))
            k_p.append(send(s_p.at[k, c], x_p.at[k, c], p_s.at[k, c], p_r.at[k, c], t, qp))

        def terms(zone, out):
            ids = lax.broadcasted_iota(jnp.int32, (prow, depth), 0) + zone * plants
            total = None
            for k in range(parts):
                if ("run", k) in loads:
                    loads.pop(("run", k)).wait()
                onehot = flags(ids == cell[:, k * depth : (k + 1) * depth]).astype(BF16)
                term = dot(onehot, run[k * depth : (k + 1) * depth, :])
                total = term if total is None else total + term
            for c in range(chunks):
                out[c] = total[:, lanes(c)]

        loads["av"].wait()
        loads["dc"].wait()
        row = price_row(lambda c: dc[:, lanes(c)])
        loads["ds"].wait()

        pl.semaphore_wait(barrier, mid + 7)
        k_ct = send(r_cto, x_ct, ct_s, ct_r, t, qn)
        k_ds = [send(ds.at[:, pl.ds(0, W)], x_ds.at[0], ds_s.at[0], ds_r.at[0], tp, q)]
        price_first(0, row)
        terms(far_zone, far)
        k_far = []

        def send_far(c):
            k_far.append(
                send(far.at[c, pl.ds(0, srow)], x_far.at[c], far_s.at[c], far_r.at[c], t, far_to)
            )

        loads["bal"].wait()
        k_ct.wait_recv()
        for i in range(cuts // W):
            place(T0 + i * W, x_ct[:, i * W : (i + 1) * W], None)
        for c in range(chunks):
            send_prices(0, c, split(bal[:, lanes(c)]))
        for c in range(chunks):
            send_far(c)

        def bound(v, b):
            return jnp.minimum(jnp.maximum(v, -b), b)

        def line_step(c, value, flow, flow_out):
            diff = joined(dot(inc[L0:P0, :], value))
            cap = colf[c_line : c_line + lines, :]
            old = flow[:, lanes(c)]
            new = bound(old + PRIMAL * diff[:lines], cap)
            bars[c, L0 : L0 + lines, :] = split(2.0 * new - old)
            flow_out[:, lanes(c)] = new
            dcut[:, lanes(c)] = diff[lines:]

        def cut_step(k, c, flow, flow_out):
            k_p[k * chunks + c].wait_recv()
            cap = colf[c_cut : c_cut + cuts, :]
            old = flow[:, lanes(c)]
            new = bound(old + PRIMAL * (x_p[k, c] + dcut[:, lanes(c)]), cap)
            bar = 2.0 * new - old
            flow_out[:, lanes(c)] = new
            s_b[k, c] = bar
            k_b.append(send(s_b.at[k, c], x_b.at[k, c], b_s.at[k, c], b_r.at[k, c], t, qn))
            bars[c, F0 : F0 + cuts, :] = split(bar)

        def cut_in(k, c, out_ref):
            k_b[k * chunks + c].wait_recv()
            more = joined(dot(inct[:, T0:rows], split(x_b[k, c])))
            out_ref[:, lanes(c)] = out_ref[:, lanes(c)] - DUAL * more

        def plant_prices(c, value):
            return joined(dot(inc[P0 : P0 + pad, :], value))[:plants]

        def release_step(c, price, old_ref, dual_ref, out_ref):
            old = old_ref[:, lanes(c)]
            new = jnp.maximum(0.0, old + PRIMAL * (price + dual_ref[:, lanes(c)]))
            bar = 2.0 * new - old
            out_ref[:, lanes(c)] = new
            padr[0:plants, :] = bar
            bars[c, P0 : P0 + pad, :] = split(padr[...])
            return bar

        def gen_step(c, old_ref, price_ref, dual_ref, out_ref):
            cost = colf[c_gen : c_gen + buses, :]
            old = old_ref[:, lanes(c)]
            new = jnp.maximum(
                0.0, old - PRIMAL * (cost - price_ref[:, lanes(c)] + dual_ref[:, lanes(c)])
            )
            gbar[:, lanes(c)] = 2.0 * new - old
            out_ref[:, lanes(c)] = new

        lane = lax.broadcasted_iota(jnp.int32, (plants, W), 1)

        def level_step(k, dual_ref, old_ref, out_ref):
            cap = colf[c_sto : c_sto + pad, :][:plants]
            rolled = [pltpu.roll(dual_ref[:, lanes(c)], W - 1, 1) for c in range(chunks)]
            rolled.append(pltpu.roll(x_ds[k], W - 1, 1))
            for c in range(chunks):
                after = jnp.where(lane == W - 1, rolled[c + 1], rolled[c])
                old = old_ref[:, lanes(c)]
                new = jnp.minimum(
                    jnp.maximum(old + PRIMAL * (dual_ref[:, lanes(c)] - after), 0.0), cap
                )
                lbar[k, :, lanes(c)] = 2.0 * new - old
                out_ref[:, lanes(c)] = new
            return send(
                lbar.at[k, :, pl.ds(hours - W, W)], x_lb.at[k], lb_s.at[k], lb_r.at[k], tn, q
            )

        def storage_step(k, dual_ref, relbars, out_ref):
            rolled = [pltpu.roll(x_lb[k], 1, 1)]
            rolled += [pltpu.roll(lbar[k, :, lanes(c)], 1, 1) for c in range(chunks)]
            for c in range(chunks):
                before = jnp.where(lane == 0, rolled[c], rolled[c + 1])
                inflow = own[c][:plants]
                out_ref[:, lanes(c)] = dual_ref[:, lanes(c)] + DUAL * (
                    inflow - lbar[k, :, lanes(c)] + before - relbars(c)
                )

        def balance_step(c, old_ref, out_ref):
            balance = gbar[:, lanes(c)] + joined(dot(inct[:, 0:T0], bars[c]))
            out_ref[:, lanes(c)] = old_ref[:, lanes(c)] + DUAL * (dem[:, lanes(c)] - balance)

        def cap_dual_step(cap_bar, dual_ref, out_ref):
            col = columns(cap_bar)
            for c in range(chunks):
                out_ref[:, lanes(c)] = jnp.maximum(
                    0.0,
                    dual_ref[:, lanes(c)] - DUAL * (av[:, lanes(c)] * col - gbar[:, lanes(c)]),
                )

        def send_inflow(c):
            k_far[c].wait_recv()
            near[c, 0:srow, :] = near[c, 0:srow, :] + x_far[c]
            k_inf.append(
                send(near.at[c, pl.ds(0, srow)], x_inf.at[c], inf_s.at[c], inf_r.at[c], t, mate)
            )

        k_inf = []
        loads["lf"].wait()
        for c in range(chunks):
            line_step(c, split(bal[:, lanes(c)]), lf, o_lf)
        loads["gen"].wait()
        for c in range(chunks):
            gen_step(c, gen, bal, dc, o_gen)
        loads["cf"].wait()
        cut_step(0, 0, cf, o_cf)
        loads["rel"].wait()
        for c in range(chunks):
            release_step(c, plant_prices(c, split(bal[:, lanes(c)])), rel, ds, o_rel)
        loads["dem"].wait()
        for c in range(chunks):
            if c:
                cut_step(0, c, cf, o_cf)
            balance_step(c, bal, o_bal)
        for c in range(chunks):
            cut_in(0, c, o_bal)
            send_prices(1, c, split(o_bal[:, lanes(c)]))
        terms(mate, near)
        for c in range(chunks):
            send_inflow(c)
        price_second(0)

        for c in range(chunks):
            line_step(c, split(o_bal[:, lanes(c)]), o_lf, o_lf)
        cut_step(1, 0, o_cf, o_cf)
        loads["lev"].wait()
        k_ds[0].wait_recv()
        k_lb = [level_step(0, ds, lev, o_lev)]
        cut_step(1, 1, o_cf, o_cf)
        cost = r_ccost[...]
        cap_old = r_cap[...]
        cap_one = jnp.maximum(0.0, cap_old - cap_step * (cost - price_all(0)))
        cap_dual_step(2.0 * cap_one - cap_old, dc, o_dc)
        cut_step(1, 2, o_cf, o_cf)
        price_first(1, price_row(lambda c: o_dc[:, lanes(c)]))
        for c in range(chunks):
            gen_step(c, o_gen, o_bal, o_dc, o_gen)
        terms(q, own)
        price_second(1)
        for c in range(chunks):
            k_inf[c].wait_recv()
            own[c, 0:srow, :] = own[c, 0:srow, :] + x_inf[c]
        k_lb[0].wait_recv()
        storage_step(0, ds, lambda c: 2.0 * o_rel[:, lanes(c)] - rel[:, lanes(c)], o_ds)
        k_ds.append(send(o_ds.at[:, pl.ds(0, W)], x_ds.at[1], ds_s.at[1], ds_r.at[1], tp, q))
        relbar = [
            release_step(c, plant_prices(c, split(o_bal[:, lanes(c)])), o_rel, o_ds, o_rel)
            for c in range(chunks)
        ]
        k_ds[1].wait_recv()
        k_lb.append(level_step(1, o_ds, o_lev, o_lev))
        for c in range(chunks):
            balance_step(c, o_bal, o_bal)
        cap_two = jnp.maximum(0.0, cap_one - cap_step * (cost - price_all(1)))
        o_cap[...] = cap_two
        cap_dual_step(2.0 * cap_two - cap_one, o_dc, o_dc)
        for c in range(chunks):
            cut_in(1, c, o_bal)
        k_lb[1].wait_recv()
        k_ds[1].wait_send()
        storage_step(1, o_ds, lambda c: relbar[c], o_ds)
        for copy in sent:
            if copy is not k_ds[1]:
                copy.wait_send()

    def big(n, kind=F32):
        return pltpu.VMEM((n, hours), kind)

    dma = pltpu.SemaphoreType.DMA
    def row(n, kind=F32):
        return pltpu.VMEM((1, n), kind)

    def lrow(kind):
        return pltpu.VMEM((lines // W, W), kind)

    i32 = jnp.int32
    scratch = [
        row(cells, i32), row(plants, i32), row(plants), lrow(i32), lrow(i32), lrow(F32),
        row(cuts, i32), row(cuts, i32), row(cuts), row(buses), row(buses), row(buses),
        big(buses), big(buses), big(cells, BF16), big(buses), big(plants), big(plants),
        big(lines), big(cuts), big(buses), big(buses), big(plants),
        pltpu.VMEM((rows, buses), BF16),
        pltpu.VMEM((buses, rows), BF16),
        pltpu.VMEM((chunks, rows - cuts, 2 * W), BF16),
        big(buses),
        pltpu.VMEM((2, plants, hours), F32),
        pltpu.VMEM((c_rows, W), F32),
        pltpu.VMEM((pad, W), F32),
        row(pad, i32), row(pad),
        big(cuts),
        pltpu.VMEM((chunks, prow, W), F32),
        pltpu.VMEM((chunks, prow, W), F32),
        pltpu.VMEM((chunks, prow, W), F32),
        pltpu.VMEM((1, cuts), jnp.int32),
        pltpu.VMEM((2, plants, W), F32),
        pltpu.VMEM((2, plants, W), F32),
        pltpu.VMEM((2, chunks, cuts, W), F32),
        pltpu.VMEM((2, chunks, cuts, W), F32),
        pltpu.VMEM((2, chunks, cuts, W), F32),
        pltpu.VMEM((2, chunks, cuts, W), F32),
        pltpu.VMEM((chunks, srow, W), F32),
        pltpu.VMEM((chunks, srow, W), F32),
        pltpu.VMEM((2, 4, 1, buses), F32),
        pltpu.VMEM((2, mid, 1, buses), F32),
        dma((22 + parts,)),
        dma, dma, dma((2,)), dma((2,)), dma((2,)), dma((2,)),
        dma((2, chunks)), dma((2, chunks)), dma((2, chunks)), dma((2, chunks)),
        dma((chunks,)), dma((chunks,)), dma((chunks,)), dma((chunks,)),
        dma((2,)), dma((2,)), dma((2,)), dma((2,)),
    ]
    return kernel, scratch


def write_out(*refs):
    count = len(refs) // 2
    sem = refs[-1]
    copies = [
        pltpu.make_async_copy(refs[i], refs[count + i], sem.at[i]) for i in range(count)
    ]
    for copy in copies:
        copy.start()
    for copy in copies:
        copy.wait()


def solution(mesh):
    times, zones = mesh.shape["tm"], mesh.shape["net"]

    def local(
        demand, availability, gen_cost, cap_cost, runoff, cell_plant, plant_bus, store_cap,
        line_from, line_to, line_cap, cut_from, cut_to, cut_cap, generation, capacity,
        release, storage_level, line_flow, cut_flow, dual_bal, dual_cap, dual_sto,
    ):
        buses, hours = demand.shape
        plants, lines, cuts, cells = (
            release.shape[0], line_flow.shape[0], cut_flow.shape[0], runoff.shape[0],
        )
        kernel, scratch = make_kernel((buses, plants, lines, cuts, cells, hours, times, zones))
        hbm = pl.BlockSpec(memory_space=pltpu.HBM)
        shapes = [(n, hours) for n in (buses, 0, plants, plants, lines, cuts, buses, buses, plants)]
        shapes[1] = (1, buses)

        def row(values):
            return values.reshape(1, -1)

        def tiles(values):
            return values.reshape(-1, W)

        outs = pl.pallas_call(
            kernel,
            out_shape=tuple(pltpu.VMEM(shape, F32) for shape in shapes),
            in_specs=[hbm] * 23,
            out_specs=(pl.BlockSpec(memory_space=pltpu.VMEM),) * 9,
            scratch_shapes=scratch,
            compiler_params=pltpu.CompilerParams(
                collective_id=0, has_side_effects=True, vmem_limit_bytes=59 << 20
            ),
        )(
            row(cell_plant), row(plant_bus), row(store_cap), tiles(line_to), tiles(line_from),
            tiles(line_cap), row(cut_from), row(cut_to), row(cut_cap), row(gen_cost), row(cap_cost),
            row(capacity),
            demand, availability, runoff, generation, release, storage_level, line_flow, cut_flow,
            dual_bal, dual_cap, dual_sto,
        )
        outs = pl.pallas_call(
            write_out,
            out_shape=tuple(jax.ShapeDtypeStruct(shape, F32) for shape in shapes),
            in_specs=[pl.BlockSpec(memory_space=pl.ANY)] * 9,
            out_specs=(hbm,) * 9,
            scratch_shapes=[pltpu.SemaphoreType.DMA((9,))],
            compiler_params=pltpu.CompilerParams(vmem_limit_bytes=1 << 20),
        )(*outs)
        outs = list(outs)
        outs[1] = outs[1].reshape(buses)
        return tuple(outs)

    both, net = P("net", "tm"), P("net")
    in_specs = (both, both, net, net, both) + (net,) * 9 + (both, net) + (both,) * 7
    out_specs = (both, net) + (both,) * 7
    return jax.shard_map(local, mesh=mesh, in_specs=in_specs, out_specs=out_specs, check_vma=False)
```
